32 devices in a mesh: image: 8 (over z, x), domain: 4 (over y, core).
Axes of the slice: x: 2, y: 2, z: 4, core: 2. Of those that a mesh axis runs over, the one named last changes fastest.
Arguments:
- field: float32 [8, 16, 64, 128], P('image', 'domain'), may hold values from -0.9 to 1.1
- mobility: float32 [16, 64, 128], P('domain'), may hold values from 0.2 to 1
- lower: int32 [2, 8], P(None, 'image'), may hold values from 0 to 6, as said below
- weights: float32 [2, 8], P(None, 'image'), may hold values from 0 to 1
Outputs:
- evolved: float32 [8, 16, 64, 128], P('image', 'domain')
- arclength: float32 [2, 8], P(None, 'image')
The draws below stay inside these ranges and needn't reach their ends.
Inputs may be any that keep to these rules, and one draw needn't show every extreme that they name: lower[c, i] is i - 1 or i.
All inputs are finite; a program needn't handle non-finite values.
Results may differ from the reference program's by a relative error of at most 0.0001.
Values sent between devices are 32-bit elements; how exact they have to be, the bound alone decides.
A program may use at most 64 MiB of HBM per device.

```python
import math
import jax
import jax.numpy as jnp
from jax import lax

NY = 64
NZ = 128
STEPS = 8
CYCLES = 2
IMAGES = 8
NX = 16


def draw_field(key, part):
    ramp_level = jnp.arange(NX, dtype=jnp.float32) / (NX - 1)
    random_part = jax.random.uniform(key, (IMAGES, NX, NY, NZ), jnp.float32, -1.0, 1.0)
    amplitude = 0.3 + 0.6 * ramp_level
    return amplitude[None, :, None, None] * random_part


def draw_lower(key, part):
    offsets = jax.random.randint(jax.random.fold_in(key, 7), (CYCLES, IMAGES), 0, 2)
    image_number = jnp.arange(IMAGES, dtype=jnp.int32)[None, :]
    return jnp.clip(image_number - 1 + offsets, 0, IMAGES - 2).astype(jnp.int32)


def steps_of(own_key, shape, split, least, largest):
    def one(dim, shards_of):
        draws = jax.random.uniform(jax.random.fold_in(jax.random.fold_in(own_key, 6), dim), (shards_of,), jnp.float32, least / len(split), largest / len(split))
        return jnp.repeat(jnp.exp(draws), shape[dim] // shards_of).reshape((-1,) + (1,) * (len(shape) - dim - 1))

    loudness = one(*split[0])
    for cut in split[1:]:
        loudness = loudness * one(*cut)
    return loudness


def setup_inputs(seed: int = 0) -> dict:
    key_of = jax.random.split(jax.random.key(seed), 5)
    field = draw_field(jax.random.fold_in(key_of[4], 71), 0)
    mobility = jnp.clip(jnp.exp(math.log(1.0) - 1.609438 * jax.random.uniform(key_of[1], (NX, NY, NZ), jnp.float32) ** steps_of(key_of[1], (NX, NY, NZ), ((0, 4),), -0.2, 0.2)), 0.2, 1.0)
    lower = draw_lower(jax.random.fold_in(key_of[4], 71), 0)
    weights = jnp.clip(1.0 * jax.random.uniform(key_of[3], (CYCLES, IMAGES), jnp.float32) ** steps_of(key_of[3], (CYCLES, IMAGES), ((1, 8),), -0.2, 0.2), 0.0, 1.0)
    return dict(field=field, mobility=mobility, lower=lower, weights=weights)


stiffness = 1.0
time_step = 0.008
epsilon = 1e-06

def advance(padded, mobile_padded):
    interior = padded[1:-1]
    laplacian = padded[2:] + padded[:-2] + jnp.roll(interior, 1, 1) + jnp.roll(interior, -1, 1) + jnp.roll(interior, 1, 2) + jnp.roll(interior, -1, 2) - 6.0 * interior
    potential = interior * interior * interior - interior - stiffness * laplacian
    motion = mobile_padded[1:-1] / (1.0 + interior * interior)
    centre = motion[1:-1]
    middle = potential[1:-1]
    change = 0.5 * (centre + motion[2:]) * (potential[2:] - middle) + 0.5 * (centre + motion[:-2]) * (potential[:-2] - middle)
    for dimension in (1, 2):
        for offset in (1, -1):
            change = change + 0.5 * (centre + jnp.roll(centre, offset, dimension)) * (jnp.roll(middle, offset, dimension) - middle)
    return padded[2:-2] + time_step * change

def wrap_rows(array, margin):
    return jnp.concatenate([array[-margin:], array, array[:margin]], axis=0)

def evolve_image(image_field, mobility):
    mobile_padded = wrap_rows(mobility, 2)
    for repeat in range(STEPS):
        image_field = advance(wrap_rows(image_field, 2), mobile_padded)
    return image_field

def reference(field, mobility, lower, weights):
    images = field
    total_cells = NX * NY * NZ
    lengths = []
    for cycle_index in range(CYCLES):
        images = lax.map(lambda single_image: evolve_image(single_image, mobility), images)
        gaps = lax.optimization_barrier(jnp.sum(jnp.square(images[1:] - images[:-1]), axis=(1, 2, 3)))
        distance = jnp.sqrt(gaps / total_cells + epsilon)
        arclength = jnp.concatenate([jnp.zeros((1,), jnp.float32), jnp.cumsum(distance)])
        lengths.append(arclength)
        first_image = jnp.take(images, lower[cycle_index], axis=0)
        second_image = jnp.take(images, lower[cycle_index] + 1, axis=0)
        weight_now = weights[cycle_index][:, None, None, None]
        images = weight_now * first_image + (1.0 - weight_now) * second_image
    return (images, jnp.stack(lengths))
```

```python
import functools

import jax
import jax.numpy as jnp
from jax import lax
from jax.experimental import pallas as pl
from jax.experimental.pallas import tpu as pltpu
from jax.sharding import PartitionSpec as P

STEPS = 8
CYCLES = 2
SUBLANES = 8

stiffness = 1.0
time_step = 0.008
epsilon = 1e-06
MESH = pl.DeviceIdType.MESH


def kernel(
    domain_count,
    image_count,
    field_ref,
    mobility_ref,
    lower_ref,
    weights_ref,
    evolved_ref,
    arclength_ref,
    stage,
    ring,
    potential,
    motion,
    partner_field,
    relay_field,
    sums,
    distances,
    stage_sem,
    gather_send,
    gather_recv,
    partner_send,
    partner_recv,
    relay_send,
    relay_recv,
    sum_send,
    sum_recv,
    distance_send,
    distance_recv,
):
    planes, ny, nz = stage.shape[1:]
    rows = ny // SUBLANES
    window = domain_count * planes
    crossings = domain_count // 2 - 1
    image = lax.axis_index("image")
    domain = lax.axis_index("domain")

    field_copy = pltpu.make_async_copy(field_ref.at[0], stage.at[0], stage_sem.at[0])
    mobility_copy = pltpu.make_async_copy(mobility_ref, stage.at[1], stage_sem.at[1])
    field_copy.start()
    mobility_copy.start()

    barrier = pltpu.get_barrier_semaphore()
    for away in range(1, domain_count):
        pl.semaphore_signal(barrier, inc=1, device_id=(image, lax.rem(domain + away, domain_count)), device_id_type=MESH)
    for away in range(1, image_count):
        pl.semaphore_signal(barrier, inc=1, device_id=(lax.rem(image + away, image_count), domain), device_id_type=MESH)

    domain_parity = lax.rem(domain, 2)
    sibling = domain + 1 - 2 * domain_parity
    at_sibling = lax.rem(domain - sibling + domain_count, domain_count)

    def gather_copy(buffer, message, plane):
        if message == 0:
            source, target, slot = 0, sibling, at_sibling
        elif message <= crossings:
            hop = 2 * message
            source, target, slot = 0, lax.rem(domain + hop, domain_count), domain_count - hop
        else:
            hop = 2 * (message - crossings)
            source, target = domain_count - hop, sibling
            slot = lax.rem(at_sibling + domain_count - hop, domain_count)
        return pltpu.make_async_remote_copy(
            src_ref=ring.at[buffer, source * planes + plane],
            dst_ref=ring.at[buffer, slot * planes + plane],
            send_sem=gather_send.at[buffer, message, plane],
            recv_sem=gather_recv.at[buffer, message, plane],
            device_id=(image, target),
            device_id_type=MESH,
        )

    def send_own(buffer, plane):
        for message in range(crossings, -1, -1):
            gather_copy(buffer, message, plane).start()

    def forward(buffer):
        for plane in range(planes):
            for message in range(1, crossings + 1):
                gather_copy(buffer, message, plane).wait_recv()
                gather_copy(buffer, crossings + message, plane).start()

    def finish_gather(buffer):
        for plane in range(planes):
            gather_copy(buffer, 0, plane).wait_recv()
            for message in range(crossings + 1, 2 * crossings + 1):
                gather_copy(buffer, message, plane).wait_recv()

    def drain_gather(buffer):
        for plane in range(planes):
            for message in range(2 * crossings + 1):
                gather_copy(buffer, message, plane).wait_send()

    def load_interleaved(which, buffer):
        for plane in range(planes):
            for row in range(rows):
                ring[buffer, plane, row] = stage[which, plane, pl.ds(row, SUBLANES, stride=rows), :]

    field_copy.wait()
    load_interleaved(0, 0)
    mobility_copy.wait()
    load_interleaved(1, CYCLES)
    pl.semaphore_wait(barrier, domain_count - 1 + image_count - 1)
    for plane in range(planes):
        send_own(0, plane)
    for plane in range(planes):
        send_own(CYCLES, plane)
    forward(0)
    forward(CYCLES)

    def next_row(value):
        return jnp.concatenate([value[1:], pltpu.roll(value[:1], SUBLANES - 1, 1)], axis=0)

    def previous_row(value):
        return jnp.concatenate([pltpu.roll(value[-1:], 1, 1), value[:-1]], axis=0)

    def next_column(value):
        return pltpu.roll(value, nz - 1, 2)

    def previous_column(value):
        return pltpu.roll(value, 1, 2)

    def advance(buffer):
        def step(number, carry):
            reach = 2 * (STEPS - 1 - number)
            offset = (2 * STEPS // window + 1) * window

            def place(index):
                return lax.rem(index, window)

            def potentials(group, carry):
                base = offset - reach - 1 + group * planes
                layers = [ring[buffer, place(base - 1 + k)] for k in range(planes + 2)]
                for k in range(planes):
                    here = layers[k + 1]
                    around = (layers[k] + layers[k + 2]) + (next_row(here) + previous_row(here))
                    around = around + (next_column(here) + previous_column(here))
                    square = here * here
                    potential[place(base + k)] = here * (square + (6.0 * stiffness - 1.0)) - stiffness * around
                    below = 1.0 + square
                    inverse = pl.reciprocal(below, approx=True)
                    inverse = inverse * (2.0 - below * inverse)
                    motion[place(base + k)] = ring[CYCLES, place(base + k)] * inverse
                return carry

            def changes(group, carry):
                base = offset - reach + group * planes
                level = [potential[place(base - 1 + k)] for k in range(planes + 2)]
                speed = [motion[place(base - 1 + k)] for k in range(planes + 2)]
                flux = [(speed[k] + speed[k + 1]) * (level[k + 1] - level[k]) for k in range(planes + 1)]
                for k in range(planes):
                    here, mobile = level[k + 1], speed[k + 1]
                    along_row = (mobile + next_row(mobile)) * (next_row(here) - here)
                    along_column = (mobile + next_column(mobile)) * (next_column(here) - here)
                    change = (flux[k + 1] - flux[k]) + (along_row - previous_row(along_row))
                    change = change + (along_column - previous_column(along_column))
                    ring[buffer, place(base + k)] = ring[buffer, place(base + k)] + (0.5 * time_step) * change
                return carry

            potential_groups = jnp.minimum(domain_count, (2 * planes + 2 * reach + 1) // planes)
            change_groups = jnp.minimum(domain_count, (2 * planes + 2 * reach - 1) // planes)
            lax.fori_loop(0, potential_groups, potentials, 0)
            lax.fori_loop(0, change_groups, changes, 0)
            return carry

        lax.fori_loop(0, STEPS, step, 0)

    image_parity = lax.rem(image, 2)
    odd = image_parity == 1
    partner = image + 1 - 2 * image_parity
    onward = image + 2 - 4 * image_parity
    has_onward = jnp.logical_and(onward >= 0, onward < image_count)
    behind = image - 2 + 4 * image_parity
    has_behind = jnp.logical_and(behind >= 0, behind < image_count)

    def partner_copy(cycle, plane):
        return pltpu.make_async_remote_copy(
            src_ref=ring.at[cycle, plane],
            dst_ref=partner_field.at[cycle, plane],
            send_sem=partner_send.at[cycle, plane],
            recv_sem=partner_recv.at[cycle, plane],
            device_id=(partner, domain),
            device_id_type=MESH,
        )

    def relay_copy(cycle, plane):
        return pltpu.make_async_remote_copy(
            src_ref=partner_field.at[cycle, plane],
            dst_ref=relay_field.at[cycle, plane],
            send_sem=relay_send.at[cycle, plane],
            recv_sem=relay_recv.at[cycle, plane],
            device_id=(onward, domain),
            device_id_type=MESH,
        )

    @pl.when(jnp.logical_not(has_behind))
    def _():
        relay_field[...] = jnp.zeros(relay_field.shape, jnp.float32)

    for cycle in range(CYCLES):
        finish_gather(cycle)
        if cycle == 0:
            finish_gather(CYCLES)
            drain_gather(CYCLES)
        drain_gather(cycle)
        advance(cycle)
        for plane in range(planes):
            partner_copy(cycle, plane).start()
        weight = weights_ref[cycle, 0]
        from_left = lower_ref[cycle, 0] < image
        own_share = jnp.where(from_left, 1.0 - weight, weight)
        other_share = jnp.where(from_left, weight, 1.0 - weight)
        from_left = jnp.where(from_left, 1, 0)
        use_partner = jnp.full((rows, SUBLANES, nz), from_left, jnp.int32) == image_parity
        left_partner = jnp.full((rows, SUBLANES, nz), image_parity, jnp.int32) == 1
        for plane in range(planes):
            partner_copy(cycle, plane).wait_recv()

            @pl.when(has_onward)
            def _():
                relay_copy(cycle, plane).start()

        gap = jnp.zeros((SUBLANES, nz), jnp.float32)
        for plane in range(planes):
            @pl.when(has_behind)
            def _():
                relay_copy(cycle, plane).wait_recv()

            own = ring[cycle, plane]
            by_partner = partner_field[cycle, plane]
            by_relay = relay_field[cycle, plane]
            mixed = own_share * own + other_share * jnp.where(use_partner, by_partner, by_relay)
            if cycle + 1 < CYCLES:
                ring[cycle + 1, plane] = mixed
                send_own(cycle + 1, plane)
            else:
                for row in range(rows):
                    evolved_ref[0, plane, pl.ds(row, SUBLANES, stride=rows), :] = mixed[row]
            difference = own - jnp.where(left_partner, by_partner, by_relay)
            gap = gap + jnp.sum(difference * difference, axis=0)
        sums[0, cycle] = gap
        if cycle + 1 < CYCLES:
            forward(cycle + 1)

    def sum_copy(away):
        return pltpu.make_async_remote_copy(
            src_ref=sums.at[0],
            dst_ref=sums.at[away],
            send_sem=sum_send.at[away],
            recv_sem=sum_recv.at[away],
            device_id=(image, lax.rem(domain + away, domain_count)),
            device_id_type=MESH,
        )

    def distance_copy(away):
        return pltpu.make_async_remote_copy(
            src_ref=distances.at[0],
            dst_ref=distances.at[away],
            send_sem=distance_send.at[away],
            recv_sem=distance_recv.at[away],
            device_id=(image + away, domain),
            device_id_type=MESH,
        )

    for away in range(1, domain_count):
        sum_copy(away).start()
    for away in range(1, domain_count):
        sum_copy(away).wait_recv()
    total_cells = window * ny * nz
    for cycle in range(CYCLES):
        gap = sums[0, cycle]
        for away in range(1, domain_count):
            gap = gap + sums[away, cycle]
        gap = jnp.sum(jnp.sum(gap, axis=0, keepdims=True), axis=1, keepdims=True)
        distance = jnp.sqrt(gap / total_cells + epsilon)
        distance = jnp.where(jnp.full((1, 1), image, jnp.int32) == 0, 0.0, distance)
        distances[0, cycle : cycle + 1, :] = jnp.broadcast_to(distance, (1, nz))
    for away in range(1, image_count):
        @pl.when(image + away < image_count)
        def _():
            distance_copy(away).start()

    arclength_ref[...] = distances[0, :CYCLES, :1]
    for away in range(1, image_count):
        @pl.when(image >= away)
        def _():
            distance_copy(away).wait_recv()
            arclength_ref[...] = arclength_ref[...] + distances[away, :CYCLES, :1]

    for cycle in range(CYCLES):
        for plane in range(planes):
            partner_copy(cycle, plane).wait_send()

            @pl.when(has_onward)
            def _():
                relay_copy(cycle, plane).wait_send()

    for away in range(1, domain_count):
        sum_copy(away).wait_send()
    for away in range(1, image_count):
        @pl.when(image + away < image_count)
        def _():
            distance_copy(away).wait_send()


def per_device(field, mobility, lower, weights):
    domain_count = lax.axis_size("domain")
    image_count = lax.axis_size("image")
    planes, ny, nz = mobility.shape
    rows = ny // SUBLANES
    window = domain_count * planes
    messages = 2 * (domain_count // 2 - 1) + 1
    block = (planes, rows, SUBLANES, nz)
    whole = (window, rows, SUBLANES, nz)
    dma = pltpu.SemaphoreType.DMA
    anywhere = pl.BlockSpec(memory_space=pl.ANY)
    vmem = pl.BlockSpec(memory_space=pltpu.VMEM)
    smem = pl.BlockSpec(memory_space=pltpu.SMEM)
    evolved, arclength = pl.pallas_call(
        functools.partial(kernel, domain_count, image_count),
        out_shape=(
            jax.ShapeDtypeStruct(field.shape, jnp.float32),
            jax.ShapeDtypeStruct((CYCLES, 1), jnp.float32),
        ),
        in_specs=[anywhere, anywhere, smem, smem],
        out_specs=(vmem, vmem),
        scratch_shapes=[
            pltpu.VMEM((2, planes, ny, nz), jnp.float32),
            pltpu.VMEM((CYCLES + 1,) + whole, jnp.float32),
            pltpu.VMEM(whole, jnp.float32),
            pltpu.VMEM(whole, jnp.float32),
            pltpu.VMEM((CYCLES,) + block, jnp.float32),
            pltpu.VMEM((CYCLES,) + block, jnp.float32),
            pltpu.VMEM((domain_count, CYCLES, SUBLANES, nz), jnp.float32),
            pltpu.VMEM((image_count, SUBLANES, nz), jnp.float32),
            dma((2,)),
            dma((CYCLES + 1, messages, planes)),
            dma((CYCLES + 1, messages, planes)),
            dma((CYCLES, planes)),
            dma((CYCLES, planes)),
            dma((CYCLES, planes)),
            dma((CYCLES, planes)),
            dma((domain_count,)),
            dma((domain_count,)),
            dma((image_count,)),
            dma((image_count,)),
        ],
        compiler_params=pltpu.CompilerParams(collective_id=0, has_side_effects=True, vmem_limit_bytes=32 * 1024 * 1024),
    )(field, mobility, lower, weights)
    return evolved, arclength


def solution(mesh):
    return jax.shard_map(
        per_device,
        mesh=mesh,
        in_specs=(
            P("image", "domain", None, None),
            P("domain", None, None),
            P(None, "image"),
            P(None, "image"),
        ),
        out_specs=(P("image", "domain", None, None), P(None, "image")),
        check_vma=False,
    )
```

```python
import functools

import jax
import jax.numpy as jnp
from jax import lax
from jax.experimental import pallas as pl
from jax.experimental.pallas import tpu as pltpu
from jax.sharding import PartitionSpec as P

STEPS = 8
CYCLES = 2
SUBLANES = 8

stiffness = 1.0
time_step = 0.008
epsilon = 1e-06
MESH = pl.DeviceIdType.MESH


def kernel(
    domain_count,
    image_count,
    field_ref,
    mobility_ref,
    lower_hbm,
    weights_hbm,
    evolved_ref,
    arclength_ref,
    lower_ref,
    weights_ref,
    stage,
    ring,
    potential,
    motion,
    partner_field,
    relay_field,
    sums,
    distances,
    stage_sem,
    gather_send,
    gather_recv,
    partner_send,
    partner_recv,
    relay_send,
    relay_recv,
    sum_send,
    sum_recv,
    distance_send,
    distance_recv,
):
    planes, ny, nz = stage.shape[1:]
    rows = ny // SUBLANES
    window = domain_count * planes
    crossings = domain_count // 2 - 1
    image = lax.axis_index("image")
    domain = lax.axis_index("domain")

    field_copy = pltpu.make_async_copy(field_ref.at[0], stage.at[0], stage_sem.at[0])
    mobility_copy = pltpu.make_async_copy(mobility_ref, stage.at[1], stage_sem.at[1])
    field_copy.start()
    mobility_copy.start()
    lower_copy = pltpu.make_async_copy(lower_hbm, lower_ref, stage_sem.at[2])
    weights_copy = pltpu.make_async_copy(weights_hbm, weights_ref, stage_sem.at[3])
    lower_copy.start()
    weights_copy.start()

    barrier = pltpu.get_barrier_semaphore()
    for away in range(1, domain_count):
        pl.semaphore_signal(barrier, inc=1, device_id=(image, lax.rem(domain + away, domain_count)), device_id_type=MESH)
    for away in range(1, image_count):
        pl.semaphore_signal(barrier, inc=1, device_id=(lax.rem(image + away, image_count), domain), device_id_type=MESH)

    domain_parity = lax.rem(domain, 2)
    sibling = domain + 1 - 2 * domain_parity
    at_sibling = lax.rem(domain - sibling + domain_count, domain_count)

    def gather_copy(buffer, message, plane):
        if message == 0:
            source, target, slot = 0, sibling, at_sibling
        elif message <= crossings:
            hop = 2 * message
            source, target, slot = 0, lax.rem(domain + hop, domain_count), domain_count - hop
        else:
            hop = 2 * (message - crossings)
            source, target = domain_count - hop, sibling
            slot = lax.rem(at_sibling + domain_count - hop, domain_count)
        return pltpu.make_async_remote_copy(
            src_ref=ring.at[buffer, source * planes + plane],
            dst_ref=ring.at[buffer, slot * planes + plane],
            send_sem=gather_send.at[buffer, message, plane],
            recv_sem=gather_recv.at[buffer, message, plane],
            device_id=(image, target),
            device_id_type=MESH,
        )

    def send_own(buffer, plane):
        for message in range(crossings, -1, -1):
            gather_copy(buffer, message, plane).start()

    def forward(buffer):
        for plane in range(planes):
            for message in range(1, crossings + 1):
                gather_copy(buffer, message, plane).wait_recv()
                gather_copy(buffer, crossings + message, plane).start()

    def finish_gather(buffer):
        for plane in range(planes):
            gather_copy(buffer, 0, plane).wait_recv()
            for message in range(crossings + 1, 2 * crossings + 1):
                gather_copy(buffer, message, plane).wait_recv()

    def drain_gather(buffer):
        for plane in range(planes):
            for message in range(2 * crossings + 1):
                gather_copy(buffer, message, plane).wait_send()

    def load_interleaved(which, buffer):
        for plane in range(planes):
            for row in range(rows):
                ring[buffer, plane, row] = stage[which, plane, pl.ds(row, SUBLANES, stride=rows), :]

    field_copy.wait()
    load_interleaved(0, 0)
    mobility_copy.wait()
    load_interleaved(1, CYCLES)
    pl.semaphore_wait(barrier, domain_count - 1 + image_count - 1)
    for plane in range(planes):
        send_own(0, plane)
    for plane in range(planes):
        send_own(CYCLES, plane)
    forward(0)
    forward(CYCLES)

    def next_row(value):
        return jnp.concatenate([value[1:], pltpu.roll(value[:1], SUBLANES - 1, 1)], axis=0)

    def previous_row(value):
        return jnp.concatenate([pltpu.roll(value[-1:], 1, 1), value[:-1]], axis=0)

    def next_column(value):
        return pltpu.roll(value, nz - 1, 2)

    def previous_column(value):
        return pltpu.roll(value, 1, 2)

    def span(width, reach):
        if width + 2 * reach >= window:
            return list(range(window))
        return [index % window for index in range(-reach, width + reach)]

    def sweep(buffer, reach):
        for index in span(planes, reach + 1):
            here = ring[buffer, index]
            around = ring[buffer, (index + 1) % window] + ring[buffer, (index - 1) % window]
            around = around + (next_row(here) + previous_row(here))
            around = around + (next_column(here) + previous_column(here))
            square = here * here
            potential[index] = here * (square + (6.0 * stiffness - 1.0)) - stiffness * around
            below = 1.0 + square
            inverse = pl.reciprocal(below, approx=True)
            inverse = inverse * (2.0 - below * inverse)
            motion[index] = ring[CYCLES, index] * inverse
        order = span(planes, reach)

        def flux_after(index):
            after = (index + 1) % window
            return (motion[index] + motion[after]) * (potential[after] - potential[index])

        entering = flux_after((order[0] - 1) % window)
        for index in order:
            here, mobile = potential[index], motion[index]
            leaving = flux_after(index)
            along_row = (mobile + next_row(mobile)) * (next_row(here) - here)
            along_column = (mobile + next_column(mobile)) * (next_column(here) - here)
            change = (leaving - entering) + (along_row - previous_row(along_row))
            change = change + (along_column - previous_column(along_column))
            ring[buffer, index] = ring[buffer, index] + (0.5 * time_step) * change
            entering = leaving

    def advance(buffer):
        reaches = [2 * (STEPS - 1 - number) for number in range(STEPS)]
        full = [reach for reach in reaches if planes + 2 * reach >= window]

        def full_sweep(number, carry):
            sweep(buffer, full[0])
            return carry

        if full:
            lax.fori_loop(0, len(full), full_sweep, 0)
        for reach in reaches[len(full) :]:
            sweep(buffer, reach)

    image_parity = lax.rem(image, 2)
    odd = image_parity == 1
    partner = image + 1 - 2 * image_parity
    onward = image + 2 - 4 * image_parity
    has_onward = jnp.logical_and(onward >= 0, onward < image_count)
    behind = image - 2 + 4 * image_parity
    has_behind = jnp.logical_and(behind >= 0, behind < image_count)

    def partner_copy(cycle, plane):
        return pltpu.make_async_remote_copy(
            src_ref=ring.at[cycle, plane],
            dst_ref=partner_field.at[cycle, plane],
            send_sem=partner_send.at[cycle, plane],
            recv_sem=partner_recv.at[cycle, plane],
            device_id=(partner, domain),
            device_id_type=MESH,
        )

    def relay_copy(cycle, plane):
        return pltpu.make_async_remote_copy(
            src_ref=partner_field.at[cycle, plane],
            dst_ref=relay_field.at[cycle, plane],
            send_sem=relay_send.at[cycle, plane],
            recv_sem=relay_recv.at[cycle, plane],
            device_id=(onward, domain),
            device_id_type=MESH,
        )

    @pl.when(jnp.logical_not(has_behind))
    def _():
        relay_field[...] = jnp.zeros(relay_field.shape, jnp.float32)

    lower_copy.wait()
    weights_copy.wait()
    for cycle in range(CYCLES):
        finish_gather(cycle)
        if cycle == 0:
            finish_gather(CYCLES)
            drain_gather(CYCLES)
        drain_gather(cycle)
        advance(cycle)
        for plane in range(planes):
            partner_copy(cycle, plane).start()
        weight = weights_ref[cycle, 0]
        from_left = lower_ref[cycle, 0] < image
        own_share = jnp.where(from_left, 1.0 - weight, weight)
        other_share = jnp.where(from_left, weight, 1.0 - weight)
        from_left = jnp.where(from_left, 1, 0)
        use_partner = jnp.full((rows, SUBLANES, nz), from_left, jnp.int32) == image_parity
        left_partner = jnp.full((rows, SUBLANES, nz), image_parity, jnp.int32) == 1
        for plane in range(planes):
            partner_copy(cycle, plane).wait_recv()

            @pl.when(has_onward)
            def _():
                relay_copy(cycle, plane).start()

        gap = jnp.zeros((SUBLANES, nz), jnp.float32)
        for plane in range(planes):
            @pl.when(has_behind)
            def _():
                relay_copy(cycle, plane).wait_recv()

            own = ring[cycle, plane]
            by_partner = partner_field[cycle, plane]
            by_relay = relay_field[cycle, plane]
            mixed = own_share * own + other_share * jnp.where(use_partner, by_partner, by_relay)
            if cycle + 1 < CYCLES:
                ring[cycle + 1, plane] = mixed
                send_own(cycle + 1, plane)
            else:
                for row in range(rows):
                    evolved_ref[0, plane, pl.ds(row, SUBLANES, stride=rows), :] = mixed[row]
            difference = own - jnp.where(left_partner, by_partner, by_relay)
            gap = gap + jnp.sum(difference * difference, axis=0)
        sums[0, cycle] = gap
        if cycle + 1 < CYCLES:
            forward(cycle + 1)

    def sum_copy(away):
        return pltpu.make_async_remote_copy(
            src_ref=sums.at[0],
            dst_ref=sums.at[away],
            send_sem=sum_send.at[away],
            recv_sem=sum_recv.at[away],
            device_id=(image, lax.rem(domain + away, domain_count)),
            device_id_type=MESH,
        )

    def distance_copy(away):
        return pltpu.make_async_remote_copy(
            src_ref=distances.at[0],
            dst_ref=distances.at[away],
            send_sem=distance_send.at[away],
            recv_sem=distance_recv.at[away],
            device_id=(image + away, domain),
            device_id_type=MESH,
        )

    for away in range(1, domain_count):
        sum_copy(away).start()
    for away in range(1, domain_count):
        sum_copy(away).wait_recv()
    total_cells = window * ny * nz
    for cycle in range(CYCLES):
        gap = sums[0, cycle]
        for away in range(1, domain_count):
            gap = gap + sums[away, cycle]
        gap = jnp.sum(jnp.sum(gap, axis=0, keepdims=True), axis=1, keepdims=True)
        distance = jnp.sqrt(gap / total_cells + epsilon)
        distance = jnp.where(jnp.full((1, 1), image, jnp.int32) == 0, 0.0, distance)
        distances[0, cycle : cycle + 1, :] = jnp.broadcast_to(distance, (1, nz))
    for away in range(1, image_count):
        @pl.when(image + away < image_count)
        def _():
            distance_copy(away).start()

    arclength_ref[...] = distances[0, :CYCLES, :1]
    for away in range(1, image_count):
        @pl.when(image >= away)
        def _():
            distance_copy(away).wait_recv()
            arclength_ref[...] = arclength_ref[...] + distances[away, :CYCLES, :1]

    for cycle in range(CYCLES):
        for plane in range(planes):
            partner_copy(cycle, plane).wait_send()

            @pl.when(has_onward)
            def _():
                relay_copy(cycle, plane).wait_send()

    for away in range(1, domain_count):
        sum_copy(away).wait_send()
    for away in range(1, image_count):
        @pl.when(image + away < image_count)
        def _():
            distance_copy(away).wait_send()


def per_device(field, mobility, lower, weights):
    domain_count = lax.axis_size("domain")
    image_count = lax.axis_size("image")
    planes, ny, nz = mobility.shape
    rows = ny // SUBLANES
    window = domain_count * planes
    messages = 2 * (domain_count // 2 - 1) + 1
    block = (planes, rows, SUBLANES, nz)
    whole = (window, rows, SUBLANES, nz)
    dma = pltpu.SemaphoreType.DMA
    anywhere = pl.BlockSpec(memory_space=pl.ANY)
    vmem = pl.BlockSpec(memory_space=pltpu.VMEM)
    evolved, arclength = pl.pallas_call(
        functools.partial(kernel, domain_count, image_count),
        out_shape=(
            jax.ShapeDtypeStruct(field.shape, jnp.float32),
            jax.ShapeDtypeStruct((CYCLES, 1), jnp.float32),
        ),
        in_specs=[anywhere] * 4,
        out_specs=(vmem, vmem),
        scratch_shapes=[
            pltpu.SMEM(lower.shape, jnp.int32),
            pltpu.SMEM(weights.shape, jnp.float32),
            pltpu.VMEM((2, planes, ny, nz), jnp.float32),
            pltpu.VMEM((CYCLES + 1,) + whole, jnp.float32),
            pltpu.VMEM(whole, jnp.float32),
            pltpu.VMEM(whole, jnp.float32),
            pltpu.VMEM((CYCLES,) + block, jnp.float32),
            pltpu.VMEM((CYCLES,) + block, jnp.float32),
            pltpu.VMEM((domain_count, CYCLES, SUBLANES, nz), jnp.float32),
            pltpu.VMEM((image_count, SUBLANES, nz), jnp.float32),
            dma((4,)),
            dma((CYCLES + 1, messages, planes)),
            dma((CYCLES + 1, messages, planes)),
            dma((CYCLES, planes)),
            dma((CYCLES, planes)),
            dma((CYCLES, planes)),
            dma((CYCLES, planes)),
            dma((domain_count,)),
            dma((domain_count,)),
            dma((image_count,)),
            dma((image_count,)),
        ],
        compiler_params=pltpu.CompilerParams(collective_id=0, has_side_effects=True, vmem_limit_bytes=32 * 1024 * 1024),
    )(field, mobility, lower, weights)
    return evolved, arclength


def solution(mesh):
    return jax.shard_map(
        per_device,
        mesh=mesh,
        in_specs=(
            P("image", "domain", None, None),
            P("domain", None, None),
            P(None, "image"),
            P(None, "image"),
        ),
        out_specs=(P("image", "domain", None, None), P(None, "image")),
        check_vma=False,
    )
```

```python
import functools

import jax
import jax.numpy as jnp
from jax import lax
from jax.experimental import pallas as pl
from jax.experimental.pallas import tpu as pltpu
from jax.sharding import PartitionSpec as P

STEPS = 8
CYCLES = 2
SUBLANES = 8

stiffness = 1.0
time_step = 0.008
epsilon = 1e-06
MESH = pl.DeviceIdType.MESH


def kernel(
    domain_count,
    image_count,
    field_ref,
    mobility_ref,
    lower_hbm,
    weights_hbm,
    evolved_ref,
    arclength_ref,
    lower_ref,
    weights_ref,
    stage,
    ring,
    potential,
    motion,
    partner_field,
    relay_field,
    sums,
    distances,
    stage_sem,
    gather_send,
    gather_recv,
    partner_send,
    partner_recv,
    relay_send,
    relay_recv,
    sum_send,
    sum_recv,
    distance_send,
    distance_recv,
):
    planes, ny, nz = stage.shape[1:]
    rows = ny // SUBLANES
    window = domain_count * planes
    crossings = domain_count // 2 - 1
    image = lax.axis_index("image")
    domain = lax.axis_index("domain")

    field_copy = pltpu.make_async_copy(field_ref.at[0], stage.at[0], stage_sem.at[0])
    mobility_copy = pltpu.make_async_copy(mobility_ref, stage.at[1], stage_sem.at[1])
    field_copy.start()
    mobility_copy.start()
    lower_copy = pltpu.make_async_copy(lower_hbm, lower_ref, stage_sem.at[2])
    weights_copy = pltpu.make_async_copy(weights_hbm, weights_ref, stage_sem.at[3])
    lower_copy.start()
    weights_copy.start()

    barrier = pltpu.get_barrier_semaphore()
    for away in range(1, domain_count):
        pl.semaphore_signal(barrier, inc=1, device_id=(image, lax.rem(domain + away, domain_count)), device_id_type=MESH)
    for away in range(1, image_count):
        pl.semaphore_signal(barrier, inc=1, device_id=(lax.rem(image + away, image_count), domain), device_id_type=MESH)

    domain_parity = lax.rem(domain, 2)
    sibling = domain + 1 - 2 * domain_parity
    at_sibling = lax.rem(domain - sibling + domain_count, domain_count)

    def gather_copy(buffer, message, plane):
        if message == 0:
            source, target, slot = 0, sibling, at_sibling
        elif message <= crossings:
            hop = 2 * message
            source, target, slot = 0, lax.rem(domain + hop, domain_count), domain_count - hop
        else:
            hop = 2 * (message - crossings)
            source, target = domain_count - hop, sibling
            slot = lax.rem(at_sibling + domain_count - hop, domain_count)
        return pltpu.make_async_remote_copy(
            src_ref=ring.at[buffer, source * planes + plane],
            dst_ref=ring.at[buffer, slot * planes + plane],
            send_sem=gather_send.at[buffer, message, plane],
            recv_sem=gather_recv.at[buffer, message, plane],
            device_id=(image, target),
            device_id_type=MESH,
        )

    def send_own(buffer, plane):
        for message in range(crossings, -1, -1):
            gather_copy(buffer, message, plane).start()

    def forward(buffer):
        for plane in range(planes):
            for message in range(1, crossings + 1):
                gather_copy(buffer, message, plane).wait_recv()
                gather_copy(buffer, crossings + message, plane).start()

    def finish_gather(buffer):
        for plane in range(planes):
            gather_copy(buffer, 0, plane).wait_recv()
            for message in range(crossings + 1, 2 * crossings + 1):
                gather_copy(buffer, message, plane).wait_recv()

    def drain_gather(buffer):
        for plane in range(planes):
            for message in range(2 * crossings + 1):
                gather_copy(buffer, message, plane).wait_send()

    def load_interleaved(which, buffer):
        for plane in range(planes):
            for row in range(rows):
                ring[buffer, plane, row] = stage[which, plane, pl.ds(row, SUBLANES, stride=rows), :]

    field_copy.wait()
    load_interleaved(0, 0)
    mobility_copy.wait()
    load_interleaved(1, CYCLES)
    pl.semaphore_wait(barrier, domain_count - 1 + image_count - 1)
    for plane in range(planes):
        send_own(0, plane)
    for plane in range(planes):
        send_own(CYCLES, plane)
    forward(0)
    forward(CYCLES)

    def next_row(value):
        return jnp.concatenate([value[1:], pltpu.roll(value[:1], SUBLANES - 1, 1)], axis=0)

    def previous_row(value):
        return jnp.concatenate([pltpu.roll(value[-1:], 1, 1), value[:-1]], axis=0)

    def next_column(value):
        return pltpu.roll(value, nz - 1, 2)

    def previous_column(value):
        return pltpu.roll(value, 1, 2)

    def span(width, reach):
        if width + 2 * reach >= window:
            return list(range(window))
        return [index % window for index in range(-reach, width + reach)]

    def sweep(buffer, reach):
        def turned(index):
            here = ring[buffer, index]
            return here, next_column(here), previous_column(here)

        def settle(index, here, after, before):
            around = ring[buffer, (index + 1) % window] + ring[buffer, (index - 1) % window]
            around = around + (next_row(here) + previous_row(here))
            around = around + (after + before)
            square = here * here
            potential[index] = here * (square + (6.0 * stiffness - 1.0)) - stiffness * around
            below = 1.0 + square
            inverse = pl.reciprocal(below, approx=True)
            inverse = inverse * (2.0 - below * inverse)
            motion[index] = ring[CYCLES, index] * inverse

        order = span(planes, reach + 1)
        ready = turned(order[0])
        for number, index in enumerate(order):
            later = turned(order[number + 1]) if number + 1 < len(order) else None
            settle(index, *ready)
            ready = later

        order = span(planes, reach)

        def flux_after(index):
            after = (index + 1) % window
            return (motion[index] + motion[after]) * (potential[after] - potential[index])

        def shifted(index):
            return next_column(potential[index]), next_column(motion[index])

        def column_flux(index, level, speed):
            along = (motion[index] + speed) * (level - potential[index])
            return along, previous_column(along)

        def finish(index, entering, along, along_before):
            here, mobile = potential[index], motion[index]
            leaving = flux_after(index)
            along_row = (mobile + next_row(mobile)) * (next_row(here) - here)
            change = (leaving - entering) + (along_row - previous_row(along_row))
            change = change + (along - along_before)
            ring[buffer, index] = ring[buffer, index] + (0.5 * time_step) * change
            return leaving

        entering = flux_after((order[0] - 1) % window)
        moved, along = {}, {}
        for tick in range(len(order) + 2):
            if tick < len(order):
                moved[tick] = shifted(order[tick])
            if 1 <= tick <= len(order):
                along[tick - 1] = column_flux(order[tick - 1], *moved.pop(tick - 1))
            if tick >= 2:
                entering = finish(order[tick - 2], entering, *along.pop(tick - 2))

    def advance(buffer):
        reaches = [2 * (STEPS - 1 - number) for number in range(STEPS)]
        full = [reach for reach in reaches if planes + 2 * reach >= window]

        def full_sweep(number, carry):
            sweep(buffer, full[0])
            return carry

        if full:
            lax.fori_loop(0, len(full), full_sweep, 0)
        for reach in reaches[len(full) :]:
            sweep(buffer, reach)

    image_parity = lax.rem(image, 2)
    odd = image_parity == 1
    partner = image + 1 - 2 * image_parity
    onward = image + 2 - 4 * image_parity
    has_onward = jnp.logical_and(onward >= 0, onward < image_count)
    behind = image - 2 + 4 * image_parity
    has_behind = jnp.logical_and(behind >= 0, behind < image_count)

    def partner_copy(cycle, plane):
        return pltpu.make_async_remote_copy(
            src_ref=ring.at[cycle, plane],
            dst_ref=partner_field.at[cycle, plane],
            send_sem=partner_send.at[cycle, plane],
            recv_sem=partner_recv.at[cycle, plane],
            device_id=(partner, domain),
            device_id_type=MESH,
        )

    def relay_copy(cycle, plane):
        return pltpu.make_async_remote_copy(
            src_ref=partner_field.at[cycle, plane],
            dst_ref=relay_field.at[cycle, plane],
            send_sem=relay_send.at[cycle, plane],
            recv_sem=relay_recv.at[cycle, plane],
            device_id=(onward, domain),
            device_id_type=MESH,
        )

    @pl.when(jnp.logical_not(has_behind))
    def _():
        relay_field[...] = jnp.zeros(relay_field.shape, jnp.float32)

    lower_copy.wait()
    weights_copy.wait()
    for cycle in range(CYCLES):
        finish_gather(cycle)
        if cycle == 0:
            finish_gather(CYCLES)
            drain_gather(CYCLES)
        drain_gather(cycle)
        advance(cycle)
        for plane in range(planes):
            partner_copy(cycle, plane).start()
        shape = (rows, SUBLANES, nz)
        weight = weights_ref[0, cycle]
        from_left = lower_ref[0, cycle] < image
        own_share = jnp.where(from_left, 1.0 - weight, weight)
        other_share = jnp.where(from_left, weight, 1.0 - weight)
        use_partner = jnp.full(shape, jnp.where(from_left, 1, 0), jnp.int32) == image_parity
        left_partner = jnp.full(shape, image_parity, jnp.int32) == 1
        for plane in range(planes):
            partner_copy(cycle, plane).wait_recv()

            @pl.when(has_onward)
            def _():
                relay_copy(cycle, plane).start()

        gap = jnp.zeros((SUBLANES, nz), jnp.float32)
        for plane in range(planes):
            @pl.when(has_behind)
            def _():
                relay_copy(cycle, plane).wait_recv()

            own = ring[cycle, plane]
            by_partner = partner_field[cycle, plane]
            by_relay = relay_field[cycle, plane]
            mixed = own_share * own + other_share * jnp.where(use_partner, by_partner, by_relay)
            if cycle + 1 < CYCLES:
                ring[cycle + 1, plane] = mixed
                send_own(cycle + 1, plane)
            else:
                for row in range(rows):
                    evolved_ref[0, plane, pl.ds(row, SUBLANES, stride=rows), :] = mixed[row]
            difference = own - jnp.where(left_partner, by_partner, by_relay)
            gap = gap + jnp.sum(difference * difference, axis=0)
        sums[0, cycle] = gap
        if cycle + 1 < CYCLES:
            forward(cycle + 1)

    def sum_copy(away):
        return pltpu.make_async_remote_copy(
            src_ref=sums.at[0],
            dst_ref=sums.at[away],
            send_sem=sum_send.at[away],
            recv_sem=sum_recv.at[away],
            device_id=(image, lax.rem(domain + away, domain_count)),
            device_id_type=MESH,
        )

    def distance_copy(away):
        return pltpu.make_async_remote_copy(
            src_ref=distances.at[0],
            dst_ref=distances.at[away],
            send_sem=distance_send.at[away],
            recv_sem=distance_recv.at[away],
            device_id=(image + away, domain),
            device_id_type=MESH,
        )

    for away in range(1, domain_count):
        sum_copy(away).start()
    for away in range(1, domain_count):
        sum_copy(away).wait_recv()
    total_cells = window * ny * nz
    lane = lax.broadcasted_iota(jnp.int32, (1, nz), 1)
    by_cycle = jnp.zeros((1, nz), jnp.float32)
    for cycle in range(CYCLES):
        gap = sums[0, cycle]
        for away in range(1, domain_count):
            gap = gap + sums[away, cycle]
        gap = jnp.sum(jnp.sum(gap, axis=0, keepdims=True), axis=1, keepdims=True)
        distance = jnp.sqrt(gap / total_cells + epsilon)
        distance = jnp.where(jnp.full((1, 1), image, jnp.int32) == 0, 0.0, distance)
        by_cycle = jnp.where(lane == cycle, distance, by_cycle)
    distances[0, :1, :] = by_cycle
    for away in range(1, image_count):
        @pl.when(image + away < image_count)
        def _():
            distance_copy(away).start()

    arclength_ref[...] = distances[0, :1, :CYCLES]
    for away in range(1, image_count):
        @pl.when(image >= away)
        def _():
            distance_copy(away).wait_recv()
            arclength_ref[...] = arclength_ref[...] + distances[away, :1, :CYCLES]

    for cycle in range(CYCLES):
        for plane in range(planes):
            partner_copy(cycle, plane).wait_send()

            @pl.when(has_onward)
            def _():
                relay_copy(cycle, plane).wait_send()

    for away in range(1, domain_count):
        sum_copy(away).wait_send()
    for away in range(1, image_count):
        @pl.when(image + away < image_count)
        def _():
            distance_copy(away).wait_send()


def per_device(field, mobility, lower, weights):
    domain_count = lax.axis_size("domain")
    image_count = lax.axis_size("image")
    planes, ny, nz = mobility.shape
    rows = ny // SUBLANES
    window = domain_count * planes
    messages = 2 * (domain_count // 2 - 1) + 1
    block = (planes, rows, SUBLANES, nz)
    whole = (window, rows, SUBLANES, nz)
    dma = pltpu.SemaphoreType.DMA
    hbm = pl.BlockSpec(memory_space=pltpu.HBM)
    vmem = pl.BlockSpec(memory_space=pltpu.VMEM)
    evolved, arclength = pl.pallas_call(
        functools.partial(kernel, domain_count, image_count),
        out_shape=(
            jax.ShapeDtypeStruct(field.shape, jnp.float32),
            jax.ShapeDtypeStruct((1, CYCLES), jnp.float32),
        ),
        in_specs=[hbm] * 4,
        out_specs=(vmem, vmem),
        scratch_shapes=[
            pltpu.SMEM((1, CYCLES), jnp.int32),
            pltpu.SMEM((1, CYCLES), jnp.float32),
            pltpu.VMEM((2, planes, ny, nz), jnp.float32),
            pltpu.VMEM((CYCLES + 1,) + whole, jnp.float32),
            pltpu.VMEM(whole, jnp.float32),
            pltpu.VMEM(whole, jnp.float32),
            pltpu.VMEM((CYCLES,) + block, jnp.float32),
            pltpu.VMEM((CYCLES,) + block, jnp.float32),
            pltpu.VMEM((domain_count, CYCLES, SUBLANES, nz), jnp.float32),
            pltpu.VMEM((image_count, SUBLANES, nz), jnp.float32),
            dma((4,)),
            dma((CYCLES + 1, messages, planes)),
            dma((CYCLES + 1, messages, planes)),
            dma((CYCLES, planes)),
            dma((CYCLES, planes)),
            dma((CYCLES, planes)),
            dma((CYCLES, planes)),
            dma((domain_count,)),
            dma((domain_count,)),
            dma((image_count,)),
            dma((image_count,)),
        ],
        compiler_params=pltpu.CompilerParams(collective_id=0, has_side_effects=True, vmem_limit_bytes=63 * 1024 * 1024),
    )(field, mobility, lower.T, weights.T)
    return evolved, arclength.T


def solution(mesh):
    return jax.shard_map(
        per_device,
        mesh=mesh,
        in_specs=(
            P("image", "domain", None, None),
            P("domain", None, None),
            P(None, "image"),
            P(None, "image"),
        ),
        out_specs=(P("image", "domain", None, None), P(None, "image")),
        check_vma=False,
    )
```
